32 devices in a mesh: xy: 8 (over z, x), gz: 4 (over y, core).
Axes of the slice: x: 2, y: 2, z: 4, core: 2. Of those that a mesh axis runs over, the one named last changes fastest.
Arguments:
- observed: float32 [256, 128, 256], P('gz', 'xy'), may hold values from 0.5 to 18
- estimate: float32 [256, 128, 256], P('gz', 'xy'), may hold values from 0.5 to 8
- lateral_psf: float32 [9, 9], replicated, may hold values from 0.0075 to 1.03
- depth_psf: float32 [64], replicated, may hold values from 0.0075 to 1.03
Outputs:
- restored: float32 [256, 128, 256], P('gz', 'xy')
The draws below stay inside these ranges and needn't reach their ends.
All inputs are finite; a program needn't handle non-finite values.
Results may differ from the reference program's by a relative error of at most 0.0001.
Values sent between devices are 32-bit elements; how exact they have to be, the bound alone decides.
A program may use at most 64 MiB of HBM per device.

```python
import math
import jax
import jax.numpy as jnp
from jax import lax

NY = 256
KZ = 64
KL = 9
ITERS = 2
NX = 128
NZ = 256


def draw_observed(key, part):
    key = jax.random.fold_in(key, 11)
    key_back, key_spot, key_amp = jax.random.split(key, 3)
    shape = (NZ, NX, NY)
    background = jnp.exp(jax.random.uniform(key_back, shape, jnp.float32, math.log(0.5), math.log(2.0)))
    amplitude = jnp.exp(jax.random.uniform(key_amp, shape, jnp.float32, math.log(4.0), math.log(16.0)))
    spots = jax.random.randint(key_spot, shape, 0, 50) == 0
    return (background + jnp.where(spots, amplitude, 0.0)).astype(jnp.float32)


def draw_estimate(key, part):
    key = jax.random.fold_in(key, 12)
    key_back, key_spot, key_amp = jax.random.split(key, 3)
    shape = (NZ, NX, NY)
    background = jnp.exp(jax.random.uniform(key_back, shape, jnp.float32, math.log(0.5), math.log(2.0)))
    amplitude = jnp.exp(jax.random.uniform(key_amp, shape, jnp.float32, math.log(2.0), math.log(6.0)))
    spots = jax.random.randint(key_spot, shape, 0, 100) == 0
    return (background + jnp.where(spots, amplitude, 0.0)).astype(jnp.float32)


def draw_lateral_psf(key, part):
    key = jax.random.fold_in(key, 13)
    center = KL // 2
    rows = jnp.arange(KL, dtype=jnp.float32)[:, None] - center
    cols = jnp.arange(KL, dtype=jnp.float32)[None, :] - center
    radius_sq = rows * rows + cols * cols
    factor = jnp.exp(jax.random.uniform(key, (KL, KL), jnp.float32, math.log(0.25), 0.0))
    return (factor * (0.03 + jnp.exp(-radius_sq))).astype(jnp.float32)


def draw_depth_psf(key, part):
    key = jax.random.fold_in(key, 14)
    planes = jnp.arange(KZ, dtype=jnp.float32) - KZ // 2
    factor = jnp.exp(jax.random.uniform(key, (KZ,), jnp.float32, math.log(0.25), 0.0))
    return (factor * (0.03 + jnp.exp(-planes * planes / 2.0))).astype(jnp.float32)


def setup_inputs(seed: int = 0) -> dict:
    key_of = jax.random.split(jax.random.key(seed), 5)
    return {
        "observed": draw_observed(jax.random.fold_in(key_of[4], 71), 0),
        "estimate": draw_estimate(jax.random.fold_in(key_of[4], 71), 0),
        "lateral_psf": draw_lateral_psf(jax.random.fold_in(key_of[4], 71), 0),
        "depth_psf": draw_depth_psf(jax.random.fold_in(key_of[4], 71), 0),
    }


def lateral(volume, kernel):
    reach = kernel.shape[0] // 2
    result = lax.conv_general_dilated(volume[:, None], kernel[None, None], (1, 1), ((reach, reach), (reach, reach)), precision=lax.Precision.HIGHEST)
    return result[:, 0]


def depth_band(volume, depth_taps, offset):
    block = 128
    taps_count = depth_taps.shape[0]
    blocked = volume.reshape(volume.shape[0] // block, block, -1)
    offset_k = jnp.arange(3, dtype=jnp.int32)[:, None, None] - 1
    rows_in = jnp.arange(block, dtype=jnp.int32)[None, :, None]
    cols_out = jnp.arange(block, dtype=jnp.int32)[None, None, :]
    position = offset_k * block + rows_in - cols_out + offset
    onehot = (position[..., None] == jnp.arange(taps_count, dtype=jnp.int32)).astype(depth_taps.dtype)
    tables = jnp.einsum('kijt,t->kij', onehot, depth_taps, precision=lax.Precision.HIGHEST)
    partial_sums = jnp.einsum('kij,bic->kbjc', tables, blocked, precision=lax.Precision.HIGHEST)
    empty_block = jnp.zeros_like(partial_sums[0, :1])
    result = partial_sums[1] + jnp.concatenate([partial_sums[2, 1:], empty_block], 0) + jnp.concatenate([empty_block, partial_sums[0, :-1]], 0)
    return result.reshape(volume.shape)


def reference(observed, estimate, lateral_psf, depth_psf):
    lateral_norm = lateral_psf / jnp.sum(lateral_psf)
    depth_norm = depth_psf / jnp.sum(depth_psf)
    lateral_flip = lateral_norm[::-1, ::-1]
    depth_flip = depth_norm[::-1]
    offset = KZ // 2
    offset_flip = KZ - 1 - offset
    current = estimate
    for repeat in range(ITERS):
        blurred = depth_band(lateral(current, lateral_norm), depth_norm, offset)
        quotient = observed / blurred
        correction = lateral(depth_band(quotient, depth_flip, offset_flip), lateral_flip)
        current = current * correction
    return current
```

```python
import functools

import jax
import jax.numpy as jnp
from jax import lax
from jax.experimental import pallas as pl
from jax.experimental.pallas import tpu as pltpu
from jax.sharding import PartitionSpec as P

ITERS = 2
CHUNKS = 4
MESH = pl.DeviceIdType.MESH
F32 = jnp.float32
BF16 = jnp.bfloat16


def split(value):
    high = value.astype(BF16)
    low = (value - high.astype(F32)).astype(BF16)
    return high, low


def total_of(ref, shape):
    total = None
    if len(shape) == 1:
        for i in range(shape[0]):
            total = ref[i] if total is None else total + ref[i]
    else:
        for i in range(shape[0]):
            for j in range(shape[1]):
                total = ref[i, j] if total is None else total + ref[i, j]
    return total


def lateral_tables(psf, total, tables, flip):
    taps = psf.shape[0]
    reach = taps // 2
    cols = tables.shape[2]
    block = 64
    inverse = 1.0 / jnp.full((1, cols), total, F32)

    def step(a, carry):
        for start in range(0, cols, block):
            rows_in = lax.broadcasted_iota(jnp.int32, (block, cols), 0) + start
            cols_out = lax.broadcasted_iota(jnp.int32, (block, cols), 1)
            offset = rows_in - cols_out + reach
            band = jnp.zeros((block, cols), F32)
            for b in range(taps):
                tap = psf[taps - 1 - a, taps - 1 - b] if flip else psf[a, b]
                band = jnp.where(offset == b, tap, band)
            high, low = split(band * inverse)
            tables[a, start : start + block, :] = high
            tables[a, cols + start : cols + start + block, :] = high
            tables[a, 2 * cols + start : 2 * cols + start + block, :] = low
        return carry

    lax.fori_loop(0, taps, step, 0)


def depth_tables(psf, total, table, slot, flip):
    taps = psf.shape[0]
    planes = table.shape[1] // 2
    width = table.shape[2] // 2
    rows = lax.broadcasted_iota(jnp.int32, (planes, width), 0)
    cols = lax.broadcasted_iota(jnp.int32, (planes, width), 1)
    tap_index = rows + taps - cols if flip else cols - rows
    band = jnp.zeros((planes, width), F32)
    for t in range(taps):
        band = jnp.where(tap_index == t, psf[t], band)
    high, low = split(band * (1.0 / jnp.full((1, width), total, F32)))
    table[slot] = jnp.concatenate(
        [
            jnp.concatenate([high, high], 1),
            jnp.concatenate([low, jnp.zeros_like(low)], 1),
        ],
        0,
    )


def kernel(
    nx, ng, obs_hbm, est_hbm, lat_psf, dep_psf, out,
    u0, u1, obs, v, q, w, xr, zr, ext_hi, ext_lo, lat_t, dep_t,
    in_sem, xs, xrs, vs, vrs, qs, qrs,
):
    rows, planes, cols = u0.shape
    reach = xr.shape[2]
    half = zr.shape[3]
    chunk = planes // CHUNKS
    xi = lax.axis_index("xy")
    gi = lax.axis_index("gz")
    has_left, has_right = xi > 0, xi < nx - 1
    has_prev, has_next = gi > 0, gi < ng - 1

    def order():
        edge = [0, rows - reach]
        return edge + [s for s in range(0, rows, reach) if s not in edge]

    est_in = {}
    obs_in = {}
    for s in order():
        for x in range(s, s + reach):
            est_in[x] = pltpu.make_async_copy(est_hbm.at[:, x, :], u0.at[x], in_sem.at[0, x])
            est_in[x].start()
    for x in range(rows):
        obs_in[x] = pltpu.make_async_copy(obs_hbm.at[:, x, :], obs.at[x], in_sem.at[1, x])
        obs_in[x].start()

    barrier = pltpu.get_barrier_semaphore()
    for there, axis, index in (
        (has_left, "xy", xi - 1), (has_right, "xy", xi + 1),
        (has_prev, "gz", gi - 1), (has_next, "gz", gi + 1),
    ):
        @pl.when(there)
        def _():
            pl.semaphore_signal(barrier, inc=1, device_id={axis: index}, device_id_type=MESH)

    for there, side in ((has_left, 0), (has_right, 1)):
        @pl.when(jnp.logical_not(there))
        def _():
            for p in range(2 * ITERS):
                xr[p, side] = jnp.zeros(xr.shape[2:], F32)

    for there, side in ((has_prev, 0), (has_next, 1)):
        @pl.when(jnp.logical_not(there))
        def _():
            for p in range(2 * ITERS):
                zr[p, side] = jnp.zeros(zr.shape[2:], F32)

    pl.semaphore_wait(
        barrier,
        has_left.astype(jnp.int32) + has_right.astype(jnp.int32)
        + has_prev.astype(jnp.int32) + has_next.astype(jnp.int32),
    )

    sent = []

    def x_copy(src, p, to_right, c):
        first = rows - reach if to_right else 0
        side = 0 if to_right else 1
        at = pl.ds(c * chunk, chunk)
        return pltpu.make_async_remote_copy(
            src_ref=src.at[pl.ds(first, reach), at, :],
            dst_ref=xr.at[p, side, :, at, :],
            send_sem=xs.at[p, side, c],
            recv_sem=xrs.at[p, side, c],
            device_id={"xy": xi + 1 if to_right else xi - 1},
            device_id_type=MESH,
        )

    def x_send(src, p, to_right, c):
        there = has_right if to_right else has_left
        copy = x_copy(src, p, to_right, c)
        sent.append((there, copy))

        @pl.when(there)
        def _():
            copy.start()

    def x_wait(src, p, c):
        for to_right, there in ((True, has_left), (False, has_right)):
            @pl.when(there)
            def _():
                x_copy(src, p, to_right, c).wait_recv()

    def v_copy(p, c):
        first = c * chunk
        to_next = first >= half
        landing = first - half if to_next else first
        return pltpu.make_async_remote_copy(
            src_ref=v.at[p, :, pl.ds(first, chunk), :],
            dst_ref=zr.at[2 * p, 0 if to_next else 1, :, pl.ds(landing, chunk), :],
            send_sem=vs.at[p, c],
            recv_sem=vrs.at[p, c],
            device_id={"gz": gi + 1 if to_next else gi - 1},
            device_id_type=MESH,
        )

    def v_send(p, c):
        there = has_next if c * chunk >= half else has_prev
        copy = v_copy(p, c)
        sent.append((there, copy))

        @pl.when(there)
        def _():
            copy.start()

    def v_wait(p):
        for c in range(CHUNKS):
            @pl.when(has_prev if c * chunk >= half else has_next)
            def _():
                v_copy(p, c).wait_recv()

    def q_copy(p, start, to_next):
        group = pl.ds(start, reach)
        side = 0 if to_next else 1
        return pltpu.make_async_remote_copy(
            src_ref=q.at[p, group, pl.ds(half if to_next else 0, half), :],
            dst_ref=zr.at[2 * p + 1, side, group, :, :],
            send_sem=qs.at[p, side, start // reach],
            recv_sem=qrs.at[p, side, start // reach],
            device_id={"gz": gi + 1 if to_next else gi - 1},
            device_id_type=MESH,
        )

    def q_send(p, start):
        for to_next, there in ((True, has_next), (False, has_prev)):
            copy = q_copy(p, start, to_next)
            sent.append((there, copy))

            @pl.when(there)
            def _():
                copy.start()

    def q_wait(p, start):
        for to_next, there in ((True, has_prev), (False, has_next)):
            @pl.when(there)
            def _():
                q_copy(p, start, to_next).wait_recv()

    def lateral(src, p, c, flip):
        at = pl.ds(c * chunk, chunk)
        slot = c % 2
        for piece, first, count in (
            (xr.at[p, 0], 0, reach), (src, reach, rows), (xr.at[p, 1], reach + rows, reach),
        ):
            high, low = split(piece[:, at, :])
            ext_hi[slot, first : first + count] = high
            ext_lo[slot, first : first + count] = low
        total = None
        for a in range(lat_t.shape[1]):
            high = ext_hi[slot, a : a + rows].reshape(rows * chunk, cols)
            low = ext_lo[slot, a : a + rows].reshape(rows * chunk, cols)
            part = jnp.dot(
                jnp.concatenate([high, low, high], 1), lat_t[flip, a], preferred_element_type=F32
            )
            total = part if total is None else total + part
        return total.reshape(rows, chunk, cols)

    def depth(src, p, x, flip):
        high, low = split(jnp.concatenate([zr[p, 0, x], src[x], zr[p, 1, x]], 0))
        both = jnp.dot(
            dep_t[flip], jnp.concatenate([high, low], 0), preferred_element_type=F32
        )
        return both[:planes] + both[planes:]

    for s in order()[:2]:
        for x in range(s, s + reach):
            est_in[x].wait()
        for c in range(CHUNKS):
            x_send(u0, 0, s > 0, c)

    lat_total = total_of(lat_psf, lat_psf.shape)
    dep_total = total_of(dep_psf, dep_psf.shape)
    for flip in (0, 1):
        lateral_tables(lat_psf, lat_total, lat_t.at[flip], flip)
        depth_tables(dep_psf, dep_total, dep_t, flip, flip)
    for s in order()[2:]:
        for x in range(s, s + reach):
            est_in[x].wait()
    for x in range(rows):
        obs_in[x].wait()

    current = u0
    for p in range(ITERS):
        for c in range(CHUNKS):
            x_wait(current, 2 * p, c)
            v[p, :, c * chunk : (c + 1) * chunk, :] = lateral(current, 2 * p, c, 0)
            v_send(p, c)
        v_wait(p)
        for s in order():
            for x in range(s, s + reach):
                q[p, x] = obs[x] / depth(v.at[p], 2 * p, x, 0)
            q_send(p, s)
        for s in order():
            q_wait(p, s)
            for x in range(s, s + reach):
                w[p, x] = depth(q.at[p], 2 * p + 1, x, 1)
            if s == 0 or s == rows - reach:
                for c in range(CHUNKS):
                    x_send(w.at[p], 2 * p + 1, s > 0, c)
        target = out if p == ITERS - 1 else u1
        for c in range(CHUNKS):
            at = slice(c * chunk, (c + 1) * chunk)
            x_wait(w.at[p], 2 * p + 1, c)
            target[:, at, :] = current[:, at, :] * lateral(w.at[p], 2 * p + 1, c, 1)
            if p < ITERS - 1:
                x_send(u1, 2 * p + 2, False, c)
                x_send(u1, 2 * p + 2, True, c)
        current = target

    for there, copy in sent:
        @pl.when(there)
        def _():
            copy.wait_send()


def body(nx, ng, observed, estimate, lateral_psf, depth_psf):
    planes, rows, cols = estimate.shape
    taps = lateral_psf.shape[0]
    reach = taps // 2
    half = depth_psf.shape[0] // 2
    chunk = planes // CHUNKS
    groups = rows // reach
    volume = (rows, planes, cols)
    dma = pltpu.SemaphoreType.DMA
    result = pl.pallas_call(
        functools.partial(kernel, nx, ng),
        out_shape=jax.ShapeDtypeStruct(volume, F32),
        in_specs=[
            pl.BlockSpec(memory_space=pl.ANY),
            pl.BlockSpec(memory_space=pl.ANY),
            pl.BlockSpec(memory_space=pltpu.SMEM),
            pl.BlockSpec(memory_space=pltpu.SMEM),
        ],
        out_specs=pl.BlockSpec(memory_space=pltpu.VMEM),
        scratch_shapes=[
            pltpu.VMEM(volume, F32),
            pltpu.VMEM(volume, F32),
            pltpu.VMEM(volume, F32),
            pltpu.VMEM((ITERS,) + volume, F32),
            pltpu.VMEM((ITERS,) + volume, F32),
            pltpu.VMEM((ITERS,) + volume, F32),
            pltpu.VMEM((2 * ITERS, 2, reach, planes, cols), F32),
            pltpu.VMEM((2 * ITERS, 2, rows, half, cols), F32),
            pltpu.VMEM((2, rows + 2 * reach, chunk, cols), BF16),
            pltpu.VMEM((2, rows + 2 * reach, chunk, cols), BF16),
            pltpu.VMEM((2, taps, 3 * cols, cols), BF16),
            pltpu.VMEM((2, 2 * planes, 2 * (planes + 2 * half)), BF16),
            dma((2, rows)),
            dma((2 * ITERS, 2, CHUNKS)),
            dma((2 * ITERS, 2, CHUNKS)),
            dma((ITERS, CHUNKS)),
            dma((ITERS, CHUNKS)),
            dma((ITERS, 2, groups)),
            dma((ITERS, 2, groups)),
        ],
        compiler_params=pltpu.CompilerParams(
            collective_id=0, has_side_effects=True, vmem_limit_bytes=48 * 1024 * 1024
        ),
        cost_estimate=pl.CostEstimate(
            flops=2 * 2 * ITERS * 3 * taps * planes * rows * cols * cols,
            bytes_accessed=3 * 4 * planes * rows * cols,
            transcendentals=0,
        ),
    )(observed, estimate, lateral_psf, depth_psf)
    return jnp.swapaxes(result, 0, 1)


def solution(mesh):
    return jax.shard_map(
        functools.partial(body, mesh.shape["xy"], mesh.shape["gz"]),
        mesh=mesh,
        in_specs=(P("gz", "xy", None), P("gz", "xy", None), P(), P()),
        out_specs=P("gz", "xy", None),
        check_vma=False,
    )
```

```python
import functools

import jax
import jax.numpy as jnp
from jax import lax
from jax.experimental import pallas as pl
from jax.experimental.pallas import tpu as pltpu
from jax.sharding import PartitionSpec as P

ITERS = 2
CHUNKS = 4
MESH = pl.DeviceIdType.MESH
F32 = jnp.float32
BF16 = jnp.bfloat16


def split(value):
    high = value.astype(BF16)
    low = (value - high.astype(F32)).astype(BF16)
    return high, low


def total_of(ref, shape):
    total = None
    if len(shape) == 1:
        for i in range(shape[0]):
            total = ref[i] if total is None else total + ref[i]
    else:
        for i in range(shape[0]):
            for j in range(shape[1]):
                total = ref[i, j] if total is None else total + ref[i, j]
    return total


def lateral_tables(psf, total, tables, flip):
    taps = psf.shape[0]
    reach = taps // 2
    cols = tables.shape[2]
    block = 64
    inverse = 1.0 / jnp.full((1, cols), total, F32)

    def step(a, carry):
        for start in range(0, cols, block):
            rows_in = lax.broadcasted_iota(jnp.int32, (block, cols), 0) + start
            cols_out = lax.broadcasted_iota(jnp.int32, (block, cols), 1)
            offset = rows_in - cols_out + reach
            band = jnp.zeros((block, cols), F32)
            for b in range(taps):
                tap = psf[taps - 1 - a, taps - 1 - b] if flip else psf[a, b]
                band = jnp.where(offset == b, tap, band)
            high, low = split(band * inverse)
            tables[a, start : start + block, :] = high
            tables[a, cols + start : cols + start + block, :] = high
            tables[a, 2 * cols + start : 2 * cols + start + block, :] = low
        return carry

    lax.fori_loop(0, taps, step, 0)


def depth_tables(psf, total, table, slot, flip):
    taps = psf.shape[0]
    planes = table.shape[1] // 2
    width = table.shape[2] // 2
    rows = lax.broadcasted_iota(jnp.int32, (planes, width), 0)
    cols = lax.broadcasted_iota(jnp.int32, (planes, width), 1)
    tap_index = rows + taps - cols if flip else cols - rows
    band = jnp.zeros((planes, width), F32)
    for t in range(taps):
        band = jnp.where(tap_index == t, psf[t], band)
    high, low = split(band * (1.0 / jnp.full((1, width), total, F32)))
    table[slot] = jnp.concatenate(
        [
            jnp.concatenate([high, high], 1),
            jnp.concatenate([low, jnp.zeros_like(low)], 1),
        ],
        0,
    )


def kernel(
    nx, ng, obs_hbm, est_hbm, lat_hbm, dep_hbm, out,
    u0, u1, obs, v, q, w, xr, zr, ext_hi, ext_lo, lat_t, dep_t,
    lat_psf, dep_psf, in_sem, psf_sem, xs, xrs, vs, vrs, qs, qrs,
):
    rows, planes, cols = u0.shape
    reach = xr.shape[2]
    half = zr.shape[3]
    chunk = planes // CHUNKS
    xi = lax.axis_index("xy")
    gi = lax.axis_index("gz")
    has_left, has_right = xi > 0, xi < nx - 1
    has_prev, has_next = gi > 0, gi < ng - 1

    def order():
        edge = [0, rows - reach]
        return edge + [s for s in range(0, rows, reach) if s not in edge]

    est_in = {}
    obs_in = {}
    for s in order():
        for x in range(s, s + reach):
            est_in[x] = pltpu.make_async_copy(est_hbm.at[:, x, :], u0.at[x], in_sem.at[0, x])
            est_in[x].start()
    lat_in = pltpu.make_async_copy(lat_hbm, lat_psf, psf_sem.at[0])
    dep_in = pltpu.make_async_copy(dep_hbm, dep_psf, psf_sem.at[1])
    lat_in.start()
    dep_in.start()
    for x in range(rows):
        obs_in[x] = pltpu.make_async_copy(obs_hbm.at[:, x, :], obs.at[x], in_sem.at[1, x])
        obs_in[x].start()

    barrier = pltpu.get_barrier_semaphore()
    for there, axis, index in (
        (has_left, "xy", xi - 1), (has_right, "xy", xi + 1),
        (has_prev, "gz", gi - 1), (has_next, "gz", gi + 1),
    ):
        @pl.when(there)
        def _():
            pl.semaphore_signal(barrier, inc=1, device_id={axis: index}, device_id_type=MESH)

    for there, side in ((has_left, 0), (has_right, 1)):
        @pl.when(jnp.logical_not(there))
        def _():
            for p in range(2 * ITERS):
                xr[p, side] = jnp.zeros(xr.shape[2:], F32)

    for there, side in ((has_prev, 0), (has_next, 1)):
        @pl.when(jnp.logical_not(there))
        def _():
            for p in range(2 * ITERS):
                zr[p, side] = jnp.zeros(zr.shape[2:], F32)

    pl.semaphore_wait(
        barrier,
        has_left.astype(jnp.int32) + has_right.astype(jnp.int32)
        + has_prev.astype(jnp.int32) + has_next.astype(jnp.int32),
    )

    sent = []

    def x_copy(src, p, to_right, c):
        first = rows - reach if to_right else 0
        side = 0 if to_right else 1
        at = pl.ds(c * chunk, chunk)
        return pltpu.make_async_remote_copy(
            src_ref=src.at[pl.ds(first, reach), at, :],
            dst_ref=xr.at[p, side, :, at, :],
            send_sem=xs.at[p, side, c],
            recv_sem=xrs.at[p, side, c],
            device_id={"xy": xi + 1 if to_right else xi - 1},
            device_id_type=MESH,
        )

    def x_send(src, p, to_right, c):
        there = has_right if to_right else has_left
        copy = x_copy(src, p, to_right, c)
        sent.append((there, copy))

        @pl.when(there)
        def _():
            copy.start()

    def x_wait(src, p, c):
        for to_right, there in ((True, has_left), (False, has_right)):
            @pl.when(there)
            def _():
                x_copy(src, p, to_right, c).wait_recv()

    def v_copy(p, c, start):
        first = c * chunk
        to_next = first >= half
        landing = first - half if to_next else first
        return pltpu.make_async_remote_copy(
            src_ref=v.at[p, pl.ds(start, reach), pl.ds(first, chunk), :],
            dst_ref=zr.at[2 * p, 0 if to_next else 1, pl.ds(start, reach), pl.ds(landing, chunk), :],
            send_sem=vs.at[p, c, start // reach],
            recv_sem=vrs.at[p, c, start // reach],
            device_id={"gz": gi + 1 if to_next else gi - 1},
            device_id_type=MESH,
        )

    def v_send(p, c):
        there = has_next if c * chunk >= half else has_prev
        for start in order():
            copy = v_copy(p, c, start)
            sent.append((there, copy))

            @pl.when(there)
            def _():
                copy.start()

    def v_wait(p, start):
        for c in range(CHUNKS):
            @pl.when(has_prev if c * chunk >= half else has_next)
            def _():
                v_copy(p, c, start).wait_recv()

    def q_copy(p, start, to_next):
        group = pl.ds(start, reach)
        side = 0 if to_next else 1
        return pltpu.make_async_remote_copy(
            src_ref=q.at[p, group, pl.ds(half if to_next else 0, half), :],
            dst_ref=zr.at[2 * p + 1, side, group, :, :],
            send_sem=qs.at[p, side, start // reach],
            recv_sem=qrs.at[p, side, start // reach],
            device_id={"gz": gi + 1 if to_next else gi - 1},
            device_id_type=MESH,
        )

    def q_send(p, start):
        for to_next, there in ((True, has_next), (False, has_prev)):
            copy = q_copy(p, start, to_next)
            sent.append((there, copy))

            @pl.when(there)
            def _():
                copy.start()

    def q_wait(p, start):
        for to_next, there in ((True, has_prev), (False, has_next)):
            @pl.when(there)
            def _():
                q_copy(p, start, to_next).wait_recv()

    def lateral(src, p, c, flip):
        at = pl.ds(c * chunk, chunk)
        slot = c % 2
        for piece, first, count in (
            (xr.at[p, 0], 0, reach), (src, reach, rows), (xr.at[p, 1], reach + rows, reach),
        ):
            high, low = split(piece[:, at, :])
            ext_hi[slot, first : first + count] = high
            ext_lo[slot, first : first + count] = low
        total = None
        for a in range(lat_t.shape[1]):
            high = ext_hi[slot, a : a + rows].reshape(rows * chunk, cols)
            low = ext_lo[slot, a : a + rows].reshape(rows * chunk, cols)
            part = jnp.dot(
                jnp.concatenate([high, low, high], 1), lat_t[flip, a], preferred_element_type=F32
            )
            total = part if total is None else total + part
        return total.reshape(rows, chunk, cols)

    def depth(src, p, x, flip):
        high, low = split(jnp.concatenate([zr[p, 0, x], src[x], zr[p, 1, x]], 0))
        both = jnp.dot(
            dep_t[flip], jnp.concatenate([high, low], 0), preferred_element_type=F32
        )
        return both[:planes] + both[planes:]

    for s in order()[:2]:
        for x in range(s, s + reach):
            est_in[x].wait()
        for c in range(CHUNKS):
            x_send(u0, 0, s > 0, c)

    lat_in.wait()
    dep_in.wait()
    lat_total = total_of(lat_psf, lat_psf.shape)
    dep_total = total_of(dep_psf, dep_psf.shape)
    for flip in (0, 1):
        lateral_tables(lat_psf, lat_total, lat_t.at[flip], flip)
        depth_tables(dep_psf, dep_total, dep_t, flip, flip)
    for s in order()[2:]:
        for x in range(s, s + reach):
            est_in[x].wait()

    current = u0
    for p in range(ITERS):
        for c in range(CHUNKS):
            x_wait(current, 2 * p, c)
            v[p, :, c * chunk : (c + 1) * chunk, :] = lateral(current, 2 * p, c, 0)
            v_send(p, c)
        def forward(s):
            v_wait(p, s)
            for x in range(s, s + reach):
                if p == 0:
                    obs_in[x].wait()
                q[p, x] = obs[x] / depth(v.at[p], 2 * p, x, 0)
            q_send(p, s)

        def backward(s):
            q_wait(p, s)
            for x in range(s, s + reach):
                w[p, x] = depth(q.at[p], 2 * p + 1, x, 1)
            if s == 0 or s == rows - reach:
                for c in range(CHUNKS):
                    x_send(w.at[p], 2 * p + 1, s > 0, c)

        groups = order()
        for s in groups[:3]:
            forward(s)
        for s in groups[:2]:
            backward(s)
        for s in groups[3:]:
            forward(s)
        for s in groups[2:]:
            backward(s)
        target = out if p == ITERS - 1 else u1
        for c in range(CHUNKS):
            at = slice(c * chunk, (c + 1) * chunk)
            x_wait(w.at[p], 2 * p + 1, c)
            target[:, at, :] = current[:, at, :] * lateral(w.at[p], 2 * p + 1, c, 1)
            if p < ITERS - 1:
                x_send(u1, 2 * p + 2, False, c)
                x_send(u1, 2 * p + 2, True, c)
        current = target

    for there, copy in sent:
        @pl.when(there)
        def _():
            copy.wait_send()


def body(nx, ng, observed, estimate, lateral_psf, depth_psf):
    planes, rows, cols = estimate.shape
    taps = lateral_psf.shape[0]
    reach = taps // 2
    half = depth_psf.shape[0] // 2
    chunk = planes // CHUNKS
    groups = rows // reach
    volume = (rows, planes, cols)
    dma = pltpu.SemaphoreType.DMA
    result = pl.pallas_call(
        functools.partial(kernel, nx, ng),
        out_shape=jax.ShapeDtypeStruct(volume, F32),
        in_specs=[
            pl.BlockSpec(memory_space=pltpu.HBM),
            pl.BlockSpec(memory_space=pltpu.HBM),
            pl.BlockSpec(memory_space=pltpu.HBM),
            pl.BlockSpec(memory_space=pltpu.HBM),
        ],
        out_specs=pl.BlockSpec(memory_space=pltpu.VMEM),
        scratch_shapes=[
            pltpu.VMEM(volume, F32),
            pltpu.VMEM(volume, F32),
            pltpu.VMEM(volume, F32),
            pltpu.VMEM((ITERS,) + volume, F32),
            pltpu.VMEM((ITERS,) + volume, F32),
            pltpu.VMEM((ITERS,) + volume, F32),
            pltpu.VMEM((2 * ITERS, 2, reach, planes, cols), F32),
            pltpu.VMEM((2 * ITERS, 2, rows, half, cols), F32),
            pltpu.VMEM((2, rows + 2 * reach, chunk, cols), BF16),
            pltpu.VMEM((2, rows + 2 * reach, chunk, cols), BF16),
            pltpu.VMEM((2, taps, 3 * cols, cols), BF16),
            pltpu.VMEM((2, 2 * planes, 2 * (planes + 2 * half)), BF16),
            pltpu.SMEM(lateral_psf.shape, F32),
            pltpu.SMEM(depth_psf.shape, F32),
            dma((2, rows)),
            dma((2,)),
            dma((2 * ITERS, 2, CHUNKS)),
            dma((2 * ITERS, 2, CHUNKS)),
            dma((ITERS, CHUNKS, groups)),
            dma((ITERS, CHUNKS, groups)),
            dma((ITERS, 2, groups)),
            dma((ITERS, 2, groups)),
        ],
        compiler_params=pltpu.CompilerParams(
            collective_id=0, has_side_effects=True, vmem_limit_bytes=63 * 1024 * 1024
        ),
        cost_estimate=pl.CostEstimate(
            flops=2 * 2 * ITERS * 3 * taps * planes * rows * cols * cols,
            bytes_accessed=3 * 4 * planes * rows * cols,
            transcendentals=0,
        ),
    )(observed, estimate, lateral_psf, depth_psf)
    return jnp.swapaxes(result, 0, 1)


def solution(mesh):
    return jax.shard_map(
        functools.partial(body, mesh.shape["xy"], mesh.shape["gz"]),
        mesh=mesh,
        in_specs=(P("gz", "xy", None), P("gz", "xy", None), P(), P()),
        out_specs=P("gz", "xy", None),
        check_vma=False,
    )
```

```python
import functools

import jax
import jax.numpy as jnp
from jax import lax
from jax.experimental import pallas as pl
from jax.experimental.pallas import tpu as pltpu
from jax.sharding import PartitionSpec as P

ITERS = 2
CHUNKS = 4
MESH = pl.DeviceIdType.MESH
F32 = jnp.float32
BF16 = jnp.bfloat16


def split(value):
    high = value.astype(BF16)
    low = (value - high.astype(F32)).astype(BF16)
    return high, low


def total_of(ref, shape):
    total = None
    if len(shape) == 1:
        for i in range(shape[0]):
            total = ref[i] if total is None else total + ref[i]
    else:
        for i in range(shape[0]):
            for j in range(shape[1]):
                total = ref[i, j] if total is None else total + ref[i, j]
    return total


def lateral_tables(psf, total, tables, flip):
    taps = psf.shape[0]
    reach = taps // 2
    cols = tables.shape[2]
    block = 64
    inverse = 1.0 / jnp.full((1, cols), total, F32)

    def step(a, carry):
        for start in range(0, cols, block):
            rows_in = lax.broadcasted_iota(jnp.int32, (block, cols), 0) + start
            cols_out = lax.broadcasted_iota(jnp.int32, (block, cols), 1)
            offset = rows_in - cols_out + reach
            band = jnp.zeros((block, cols), F32)
            for b in range(taps):
                tap = psf[taps - 1 - a, taps - 1 - b] if flip else psf[a, b]
                band = jnp.where(offset == b, tap, band)
            high, low = split(band * inverse)
            tables[a, start : start + block, :] = high
            tables[a, cols + start : cols + start + block, :] = high
            tables[a, 2 * cols + start : 2 * cols + start + block, :] = low
        return carry

    lax.fori_loop(0, taps, step, 0)


def depth_tables(psf, total, table, slot, flip):
    taps = psf.shape[0]
    planes = table.shape[1] // 2
    width = table.shape[2] // 2
    rows = lax.broadcasted_iota(jnp.int32, (planes, width), 0)
    cols = lax.broadcasted_iota(jnp.int32, (planes, width), 1)
    tap_index = rows + taps - cols if flip else cols - rows
    band = jnp.zeros((planes, width), F32)
    for t in range(taps):
        band = jnp.where(tap_index == t, psf[t], band)
    high, low = split(band * (1.0 / jnp.full((1, width), total, F32)))
    table[slot] = jnp.concatenate(
        [
            jnp.concatenate([high, high], 1),
            jnp.concatenate([low, jnp.zeros_like(low)], 1),
        ],
        0,
    )


def kernel(
    nx, ng, obs_hbm, est_hbm, lat_hbm, dep_hbm, out,
    u0, u1, obs, v, q, w, xr, zr, ext_hi, ext_lo, lat_t, dep_t,
    lat_psf, dep_psf, in_sem, psf_sem, xs, xrs, vs, vrs, qs, qrs,
):
    rows, planes, cols = u0.shape
    reach = xr.shape[2]
    half = zr.shape[3]
    chunk = planes // CHUNKS
    xi = lax.axis_index("xy")
    gi = lax.axis_index("gz")
    has_left, has_right = xi > 0, xi < nx - 1
    has_prev, has_next = gi > 0, gi < ng - 1

    def order():
        edge = [0, rows - reach]
        return edge + [s for s in range(0, rows, reach) if s not in edge]

    est_in = {}
    obs_in = {}
    for s in order():
        for x in range(s, s + reach):
            est_in[x] = pltpu.make_async_copy(est_hbm.at[:, x, :], u0.at[x], in_sem.at[0, x])
            est_in[x].start()
    lat_in = pltpu.make_async_copy(lat_hbm, lat_psf, psf_sem.at[0])
    dep_in = pltpu.make_async_copy(dep_hbm, dep_psf, psf_sem.at[1])
    lat_in.start()
    dep_in.start()
    for x in range(rows):
        obs_in[x] = pltpu.make_async_copy(obs_hbm.at[:, x, :], obs.at[x], in_sem.at[1, x])
        obs_in[x].start()

    barrier = pltpu.get_barrier_semaphore()
    for there, axis, index in (
        (has_left, "xy", xi - 1), (has_right, "xy", xi + 1),
        (has_prev, "gz", gi - 1), (has_next, "gz", gi + 1),
    ):
        @pl.when(there)
        def _():
            pl.semaphore_signal(barrier, inc=1, device_id={axis: index}, device_id_type=MESH)

    for there, side in ((has_left, 0), (has_right, 1)):
        @pl.when(jnp.logical_not(there))
        def _():
            for p in range(2 * ITERS):
                xr[p, side] = jnp.zeros(xr.shape[2:], F32)

    for there, side in ((has_prev, 0), (has_next, 1)):
        @pl.when(jnp.logical_not(there))
        def _():
            for p in range(2 * ITERS):
                zr[p, side] = jnp.zeros(zr.shape[2:], F32)

    pl.semaphore_wait(
        barrier,
        has_left.astype(jnp.int32) + has_right.astype(jnp.int32)
        + has_prev.astype(jnp.int32) + has_next.astype(jnp.int32),
    )

    sent = []

    def x_copy(src, p, to_right, c):
        first = rows - reach if to_right else 0
        side = 0 if to_right else 1
        at = pl.ds(c * chunk, chunk)
        return pltpu.make_async_remote_copy(
            src_ref=src.at[pl.ds(first, reach), at, :],
            dst_ref=xr.at[p, side, :, at, :],
            send_sem=xs.at[p, side, c],
            recv_sem=xrs.at[p, side, c],
            device_id={"xy": xi + 1 if to_right else xi - 1},
            device_id_type=MESH,
        )

    def x_send(src, p, to_right, c):
        there = has_right if to_right else has_left
        copy = x_copy(src, p, to_right, c)
        sent.append((there, copy))

        @pl.when(there)
        def _():
            copy.start()

    def x_wait(src, p, c):
        for to_right, there in ((True, has_left), (False, has_right)):
            @pl.when(there)
            def _():
                x_copy(src, p, to_right, c).wait_recv()

    def v_copy(p, c, start):
        first = c * chunk
        to_next = first >= half
        landing = first - half if to_next else first
        return pltpu.make_async_remote_copy(
            src_ref=v.at[p, pl.ds(start, reach), pl.ds(first, chunk), :],
            dst_ref=zr.at[2 * p, 0 if to_next else 1, pl.ds(start, reach), pl.ds(landing, chunk), :],
            send_sem=vs.at[p, c, start // reach],
            recv_sem=vrs.at[p, c, start // reach],
            device_id={"gz": gi + 1 if to_next else gi - 1},
            device_id_type=MESH,
        )

    def v_send(p, c, starts):
        there = has_next if c * chunk >= half else has_prev
        for start in starts:
            copy = v_copy(p, c, start)
            sent.append((there, copy))

            @pl.when(there)
            def _():
                copy.start()

    def v_wait(p, start):
        for c in range(CHUNKS):
            @pl.when(has_prev if c * chunk >= half else has_next)
            def _():
                v_copy(p, c, start).wait_recv()

    def q_copy(p, start, to_next):
        group = pl.ds(start, reach)
        side = 0 if to_next else 1
        return pltpu.make_async_remote_copy(
            src_ref=q.at[p, group, pl.ds(half if to_next else 0, half), :],
            dst_ref=zr.at[2 * p + 1, side, group, :, :],
            send_sem=qs.at[p, side, start // reach],
            recv_sem=qrs.at[p, side, start // reach],
            device_id={"gz": gi + 1 if to_next else gi - 1},
            device_id_type=MESH,
        )

    def q_send(p, start):
        for to_next, there in ((True, has_next), (False, has_prev)):
            copy = q_copy(p, start, to_next)
            sent.append((there, copy))

            @pl.when(there)
            def _():
                copy.start()

    def q_wait(p, start):
        for to_next, there in ((True, has_prev), (False, has_next)):
            @pl.when(there)
            def _():
                q_copy(p, start, to_next).wait_recv()

    def place(value, c, first, count):
        high, low = split(value)
        ext_hi[c, first : first + count] = high
        ext_lo[c, first : first + count] = low

    def blur(flip, spans, slots):
        total = None
        for a in range(lat_t.shape[1]):
            parts = []
            for ext in (ext_hi, ext_lo):
                pieces = [
                    ext[c, first + a : first + a + count].reshape(count * chunk, cols)
                    for c in slots
                    for first, count in spans
                ]
                parts.append(pieces[0] if len(pieces) == 1 else jnp.concatenate(pieces, 0))
            part = jnp.dot(
                jnp.concatenate([parts[0], parts[1], parts[0]], 1),
                lat_t[flip, a],
                preferred_element_type=F32,
            )
            total = part if total is None else total + part
        return total

    inner = rows - 2 * reach

    def blur_inner(src, slots, flip):
        for c in slots:
            place(src[:, c * chunk : (c + 1) * chunk, :], c, reach, rows)
        total = blur(flip, [(reach, inner)], slots)
        return total.reshape(len(slots), inner, chunk, cols)

    def blur_edges(p, c, flip):
        at = slice(c * chunk, (c + 1) * chunk)
        place(xr[p, 0, :, at, :], c, 0, reach)
        place(xr[p, 1, :, at, :], c, reach + rows, reach)
        total = blur(flip, [(0, reach), (rows - reach, reach)], [c])
        return total.reshape(2, reach, chunk, cols)

    def depth(src, p, x, flip):
        high, low = split(jnp.concatenate([zr[p, 0, x], src[x], zr[p, 1, x]], 0))
        both = jnp.dot(
            dep_t[flip], jnp.concatenate([high, low], 0), preferred_element_type=F32
        )
        return both[:planes] + both[planes:]

    for s in order()[:2]:
        for x in range(s, s + reach):
            est_in[x].wait()
        for c in range(CHUNKS):
            x_send(u0, 0, s > 0, c)

    lat_in.wait()
    dep_in.wait()
    lat_total = total_of(lat_psf, lat_psf.shape)
    dep_total = total_of(dep_psf, dep_psf.shape)
    for flip in (0, 1):
        lateral_tables(lat_psf, lat_total, lat_t.at[flip], flip)
        depth_tables(dep_psf, dep_total, dep_t, flip, flip)
    for s in order()[2:]:
        for x in range(s, s + reach):
            est_in[x].wait()

    current = u0
    every = list(range(CHUNKS))
    edge_groups, inner_groups = order()[:2], order()[2:]

    def planes_of(c):
        return slice(c * chunk, (c + 1) * chunk)

    def first_inner(p, src, slots):
        result = blur_inner(src, slots, 0)
        for k, c in enumerate(slots):
            v[p, reach : reach + inner, planes_of(c), :] = result[k]
            v_send(p, c, inner_groups)

    first_inner(0, u0, every)
    for p in range(ITERS):
        for c in every:
            x_wait(current, 2 * p, c)
            result = blur_edges(2 * p, c, 0)
            v[p, 0:reach, planes_of(c), :] = result[0]
            v[p, rows - reach : rows, planes_of(c), :] = result[1]
            v_send(p, c, edge_groups)

        def forward(s):
            v_wait(p, s)
            for x in range(s, s + reach):
                if p == 0:
                    obs_in[x].wait()
                q[p, x] = obs[x] / depth(v.at[p], 2 * p, x, 0)
            q_send(p, s)

        def backward(s):
            q_wait(p, s)
            for x in range(s, s + reach):
                w[p, x] = depth(q.at[p], 2 * p + 1, x, 1)
            if s == 0 or s == rows - reach:
                for c in range(CHUNKS):
                    x_send(w.at[p], 2 * p + 1, s > 0, c)

        groups = order()
        for s in groups[:3]:
            forward(s)
        for s in groups[:2]:
            backward(s)
        for s in groups[3:]:
            forward(s)
        for s in groups[2:]:
            backward(s)
        target = out if p == ITERS - 1 else u1
        result = blur_inner(w.at[p], every, 1)
        for c in every:
            at = planes_of(c)
            target[reach : reach + inner, at, :] = (
                current[reach : reach + inner, at, :] * result[c]
            )
        for c in every:
            at = planes_of(c)
            x_wait(w.at[p], 2 * p + 1, c)
            result = blur_edges(2 * p + 1, c, 1)
            for k, start in enumerate(edge_groups):
                span = slice(start, start + reach)
                target[span, at, :] = current[span, at, :] * result[k]
            if p < ITERS - 1:
                x_send(u1, 2 * p + 2, False, c)
                x_send(u1, 2 * p + 2, True, c)
                first_inner(p + 1, u1, [c])
        current = target

    for there, copy in sent:
        @pl.when(there)
        def _():
            copy.wait_send()


def body(nx, ng, observed, estimate, lateral_psf, depth_psf):
    planes, rows, cols = estimate.shape
    taps = lateral_psf.shape[0]
    reach = taps // 2
    half = depth_psf.shape[0] // 2
    chunk = planes // CHUNKS
    groups = rows // reach
    volume = (rows, planes, cols)
    dma = pltpu.SemaphoreType.DMA
    result = pl.pallas_call(
        functools.partial(kernel, nx, ng),
        out_shape=jax.ShapeDtypeStruct(volume, F32),
        in_specs=[
            pl.BlockSpec(memory_space=pltpu.HBM),
            pl.BlockSpec(memory_space=pltpu.HBM),
            pl.BlockSpec(memory_space=pltpu.HBM),
            pl.BlockSpec(memory_space=pltpu.HBM),
        ],
        out_specs=pl.BlockSpec(memory_space=pltpu.VMEM),
        scratch_shapes=[
            pltpu.VMEM(volume, F32),
            pltpu.VMEM(volume, F32),
            pltpu.VMEM(volume, F32),
            pltpu.VMEM((ITERS,) + volume, F32),
            pltpu.VMEM((ITERS,) + volume, F32),
            pltpu.VMEM((ITERS,) + volume, F32),
            pltpu.VMEM((2 * ITERS, 2, reach, planes, cols), F32),
            pltpu.VMEM((2 * ITERS, 2, rows, half, cols), F32),
            pltpu.VMEM((CHUNKS, rows + 2 * reach, chunk, cols), BF16),
            pltpu.VMEM((CHUNKS, rows + 2 * reach, chunk, cols), BF16),
            pltpu.VMEM((2, taps, 3 * cols, cols), BF16),
            pltpu.VMEM((2, 2 * planes, 2 * (planes + 2 * half)), BF16),
            pltpu.SMEM(lateral_psf.shape, F32),
            pltpu.SMEM(depth_psf.shape, F32),
            dma((2, rows)),
            dma((2,)),
            dma((2 * ITERS, 2, CHUNKS)),
            dma((2 * ITERS, 2, CHUNKS)),
            dma((ITERS, CHUNKS, groups)),
            dma((ITERS, CHUNKS, groups)),
            dma((ITERS, 2, groups)),
            dma((ITERS, 2, groups)),
        ],
        compiler_params=pltpu.CompilerParams(
            collective_id=0, has_side_effects=True, vmem_limit_bytes=63 * 1024 * 1024
        ),
        cost_estimate=pl.CostEstimate(
            flops=2 * 2 * ITERS * 3 * taps * planes * rows * cols * cols,
            bytes_accessed=3 * 4 * planes * rows * cols,
            transcendentals=0,
        ),
    )(observed, estimate, lateral_psf, depth_psf)
    return jnp.swapaxes(result, 0, 1)


def solution(mesh):
    return jax.shard_map(
        functools.partial(body, mesh.shape["xy"], mesh.shape["gz"]),
        mesh=mesh,
        in_specs=(P("gz", "xy", None), P("gz", "xy", None), P(), P()),
        out_specs=P("gz", "xy", None),
        check_vma=False,
    )
```

```python
import functools

import jax
import jax.numpy as jnp
from jax import lax
from jax.experimental import pallas as pl
from jax.experimental.pallas import tpu as pltpu
from jax.sharding import PartitionSpec as P

ITERS = 2
CHUNKS = 4
MESH = pl.DeviceIdType.MESH
F32 = jnp.float32
BF16 = jnp.bfloat16


def split(value):
    high = value.astype(BF16)
    low = (value - high.astype(F32)).astype(BF16)
    return high, low


def total_of(ref, shape):
    total = None
    if len(shape) == 1:
        for i in range(shape[0]):
            total = ref[i] if total is None else total + ref[i]
    else:
        for i in range(shape[0]):
            for j in range(shape[1]):
                total = ref[i, j] if total is None else total + ref[i, j]
    return total


def lateral_tables(psf, total, tables, flip):
    taps = psf.shape[0]
    reach = taps // 2
    cols = tables.shape[2]
    block = 64
    inverse = 1.0 / jnp.full((1, cols), total, F32)

    def step(a, carry):
        for start in range(0, cols, block):
            rows_in = lax.broadcasted_iota(jnp.int32, (block, cols), 0) + start
            cols_out = lax.broadcasted_iota(jnp.int32, (block, cols), 1)
            offset = rows_in - cols_out + reach
            band = jnp.zeros((block, cols), F32)
            for b in range(taps):
                tap = psf[taps - 1 - a, taps - 1 - b] if flip else psf[a, b]
                band = jnp.where(offset == b, tap, band)
            high, low = split(band * inverse)
            tables[a, start : start + block, :] = high
            tables[a, cols + start : cols + start + block, :] = high
            tables[a, 2 * cols + start : 2 * cols + start + block, :] = low
        return carry

    lax.fori_loop(0, taps, step, 0)


def depth_tables(psf, total, table, slot, flip):
    taps = psf.shape[0]
    planes = table.shape[1] // 2
    width = table.shape[2] // 2
    rows = lax.broadcasted_iota(jnp.int32, (planes, width), 0)
    cols = lax.broadcasted_iota(jnp.int32, (planes, width), 1)
    tap_index = rows + taps - cols if flip else cols - rows
    band = jnp.zeros((planes, width), F32)
    for t in range(taps):
        band = jnp.where(tap_index == t, psf[t], band)
    high, low = split(band * (1.0 / jnp.full((1, width), total, F32)))
    table[slot] = jnp.concatenate(
        [
            jnp.concatenate([high, high], 1),
            jnp.concatenate([low, jnp.zeros_like(low)], 1),
        ],
        0,
    )


def kernel(
    nx, ng, obs_hbm, est_hbm, lat_hbm, dep_hbm, out,
    u0, u1, obs, v, q, w, xr, zr, ext_hi, ext_lo, lat_t, dep_t,
    lat_psf, dep_psf, in_sem, psf_sem, xs, xrs, vs, vrs, qs, qrs,
):
    rows, planes, cols = u0.shape
    reach = xr.shape[2]
    half = zr.shape[3]
    chunk = planes // CHUNKS
    xi = lax.axis_index("xy")
    gi = lax.axis_index("gz")
    has_left, has_right = xi > 0, xi < nx - 1
    has_prev, has_next = gi > 0, gi < ng - 1

    def order():
        edge = [0, rows - reach]
        return edge + [s for s in range(0, rows, reach) if s not in edge]

    est_in = {}
    obs_in = {}
    for s in order():
        for x in range(s, s + reach):
            est_in[x] = pltpu.make_async_copy(est_hbm.at[:, x, :], u0.at[x], in_sem.at[0, x])
            est_in[x].start()
    lat_in = pltpu.make_async_copy(lat_hbm, lat_psf, psf_sem.at[0])
    dep_in = pltpu.make_async_copy(dep_hbm, dep_psf, psf_sem.at[1])
    lat_in.start()
    dep_in.start()
    for x in range(rows):
        obs_in[x] = pltpu.make_async_copy(obs_hbm.at[:, x, :], obs.at[x], in_sem.at[1, x])
        obs_in[x].start()

    barrier = pltpu.get_barrier_semaphore()
    for there, axis, index in (
        (has_left, "xy", xi - 1), (has_right, "xy", xi + 1),
        (has_prev, "gz", gi - 1), (has_next, "gz", gi + 1),
    ):
        @pl.when(there)
        def _():
            pl.semaphore_signal(barrier, inc=1, device_id={axis: index}, device_id_type=MESH)

    for there, side in ((has_left, 0), (has_right, 1)):
        @pl.when(jnp.logical_not(there))
        def _():
            for p in range(2 * ITERS):
                xr[p, side] = jnp.zeros(xr.shape[2:], F32)

    for there, side in ((has_prev, 0), (has_next, 1)):
        @pl.when(jnp.logical_not(there))
        def _():
            for p in range(2 * ITERS):
                zr[p, side] = jnp.zeros(zr.shape[2:], F32)

    pl.semaphore_wait(
        barrier,
        has_left.astype(jnp.int32) + has_right.astype(jnp.int32)
        + has_prev.astype(jnp.int32) + has_next.astype(jnp.int32),
    )

    sent = []

    def x_copy(src, p, to_right, c):
        first = rows - reach if to_right else 0
        side = 0 if to_right else 1
        at = pl.ds(c * chunk, chunk)
        return pltpu.make_async_remote_copy(
            src_ref=src.at[pl.ds(first, reach), at, :],
            dst_ref=xr.at[p, side, :, at, :],
            send_sem=xs.at[p, side, c],
            recv_sem=xrs.at[p, side, c],
            device_id={"xy": xi + 1 if to_right else xi - 1},
            device_id_type=MESH,
        )

    def x_send(src, p, to_right, c):
        there = has_right if to_right else has_left
        copy = x_copy(src, p, to_right, c)
        sent.append((there, copy))

        @pl.when(there)
        def _():
            copy.start()

    def x_wait(src, p, c):
        for to_right, there in ((True, has_left), (False, has_right)):
            @pl.when(there)
            def _():
                x_copy(src, p, to_right, c).wait_recv()

    def v_copy(p, c, start):
        first = c * chunk
        to_next = first >= half
        landing = first - half if to_next else first
        return pltpu.make_async_remote_copy(
            src_ref=v.at[p, pl.ds(start, reach), pl.ds(first, chunk), :],
            dst_ref=zr.at[2 * p, 0 if to_next else 1, pl.ds(start, reach), pl.ds(landing, chunk), :],
            send_sem=vs.at[p, c, start // reach],
            recv_sem=vrs.at[p, c, start // reach],
            device_id={"gz": gi + 1 if to_next else gi - 1},
            device_id_type=MESH,
        )

    def v_send(p, c, starts):
        there = has_next if c * chunk >= half else has_prev
        for start in starts:
            copy = v_copy(p, c, start)
            sent.append((there, copy))

            @pl.when(there)
            def _():
                copy.start()

    def v_wait(p, start):
        for c in range(CHUNKS):
            @pl.when(has_prev if c * chunk >= half else has_next)
            def _():
                v_copy(p, c, start).wait_recv()

    def q_copy(p, start, to_next):
        group = pl.ds(start, reach)
        side = 0 if to_next else 1
        return pltpu.make_async_remote_copy(
            src_ref=q.at[p, group, pl.ds(half if to_next else 0, half), :],
            dst_ref=zr.at[2 * p + 1, side, group, :, :],
            send_sem=qs.at[p, side, start // reach],
            recv_sem=qrs.at[p, side, start // reach],
            device_id={"gz": gi + 1 if to_next else gi - 1},
            device_id_type=MESH,
        )

    def q_send(p, start):
        for to_next, there in ((True, has_next), (False, has_prev)):
            copy = q_copy(p, start, to_next)
            sent.append((there, copy))

            @pl.when(there)
            def _():
                copy.start()

    def q_wait(p, start):
        for to_next, there in ((True, has_prev), (False, has_next)):
            @pl.when(there)
            def _():
                q_copy(p, start, to_next).wait_recv()

    def place(value, c, first, count):
        high, low = split(value)
        ext_hi[c, first : first + count] = high
        ext_lo[c, first : first + count] = low

    def blur(flip, spans, slots):
        total = None
        for a in range(lat_t.shape[1]):
            parts = []
            for ext in (ext_hi, ext_lo):
                pieces = [
                    ext[c, first + a : first + a + count].reshape(count * chunk, cols)
                    for c in slots
                    for first, count in spans
                ]
                parts.append(pieces[0] if len(pieces) == 1 else jnp.concatenate(pieces, 0))
            part = jnp.dot(
                jnp.concatenate([parts[0], parts[1], parts[0]], 1),
                lat_t[flip, a],
                preferred_element_type=F32,
            )
            total = part if total is None else total + part
        return total

    inner = rows - 2 * reach

    def blur_inner(src, slots, flip):
        for c in slots:
            place(src[:, c * chunk : (c + 1) * chunk, :], c, reach, rows)
        total = blur(flip, [(reach, inner)], slots)
        return total.reshape(len(slots), inner, chunk, cols)

    def blur_edges(p, c, flip):
        at = slice(c * chunk, (c + 1) * chunk)
        place(xr[p, 0, :, at, :], c, 0, reach)
        place(xr[p, 1, :, at, :], c, reach + rows, reach)
        total = blur(flip, [(0, reach), (rows - reach, reach)], [c])
        return total.reshape(2, reach, chunk, cols)

    def depth(src, p, x, flip):
        high, low = split(jnp.concatenate([zr[p, 0, x], src[x], zr[p, 1, x]], 0))
        both = jnp.dot(
            dep_t[flip], jnp.concatenate([high, low], 0), preferred_element_type=F32
        )
        return both[:planes] + both[planes:]

    for s in order()[:2]:
        for x in range(s, s + reach):
            est_in[x].wait()
        for c in range(CHUNKS):
            x_send(u0, 0, s > 0, c)

    lat_in.wait()
    dep_in.wait()
    lat_total = total_of(lat_psf, lat_psf.shape)
    dep_total = total_of(dep_psf, dep_psf.shape)
    for flip in (0, 1):
        lateral_tables(lat_psf, lat_total, lat_t.at[flip], flip)
        depth_tables(dep_psf, dep_total, dep_t, flip, flip)
    for s in order()[2:]:
        for x in range(s, s + reach):
            est_in[x].wait()

    current = u0
    every = list(range(CHUNKS))
    edge_groups, inner_groups = order()[:2], order()[2:]

    def planes_of(c):
        return slice(c * chunk, (c + 1) * chunk)

    def first_inner(p, src, slots):
        result = blur_inner(src, slots, 0)
        for k, c in enumerate(slots):
            v[p, reach : reach + inner, planes_of(c), :] = result[k]
            v_send(p, c, inner_groups)

    first_inner(0, u0, every)
    for p in range(ITERS):
        for c in every:
            x_wait(current, 2 * p, c)
            result = blur_edges(2 * p, c, 0)
            v[p, 0:reach, planes_of(c), :] = result[0]
            v[p, rows - reach : rows, planes_of(c), :] = result[1]
            v_send(p, c, edge_groups)

        def forward(s):
            v_wait(p, s)
            for x in range(s, s + reach):
                if p == 0:
                    obs_in[x].wait()
                q[p, x] = obs[x] / depth(v.at[p], 2 * p, x, 0)
            q_send(p, s)

        def backward(s):
            q_wait(p, s)
            for x in range(s, s + reach):
                w[p, x] = depth(q.at[p], 2 * p + 1, x, 1)
            if s == 0 or s == rows - reach:
                for c in range(CHUNKS):
                    x_send(w.at[p], 2 * p + 1, s > 0, c)

        groups = order()
        forward(groups[0])
        forward(groups[1])
        backward(groups[0])
        forward(groups[2])
        backward(groups[1])
        for s in groups[3:]:
            forward(s)
        for s in groups[2:]:
            backward(s)
        target = out if p == ITERS - 1 else u1
        result = blur_inner(w.at[p], every, 1)
        for c in every:
            at = planes_of(c)
            target[reach : reach + inner, at, :] = (
                current[reach : reach + inner, at, :] * result[c]
            )
        for c in every:
            at = planes_of(c)
            x_wait(w.at[p], 2 * p + 1, c)
            result = blur_edges(2 * p + 1, c, 1)
            for k, start in enumerate(edge_groups):
                span = slice(start, start + reach)
                target[span, at, :] = current[span, at, :] * result[k]
            if p < ITERS - 1:
                x_send(u1, 2 * p + 2, False, c)
                x_send(u1, 2 * p + 2, True, c)
                first_inner(p + 1, u1, [c])
        current = target

    for there, copy in sent:
        @pl.when(there)
        def _():
            copy.wait_send()


def body(nx, ng, observed, estimate, lateral_psf, depth_psf):
    planes, rows, cols = estimate.shape
    taps = lateral_psf.shape[0]
    reach = taps // 2
    half = depth_psf.shape[0] // 2
    chunk = planes // CHUNKS
    groups = rows // reach
    volume = (rows, planes, cols)
    dma = pltpu.SemaphoreType.DMA
    result = pl.pallas_call(
        functools.partial(kernel, nx, ng),
        out_shape=jax.ShapeDtypeStruct(volume, F32),
        in_specs=[
            pl.BlockSpec(memory_space=pltpu.HBM),
            pl.BlockSpec(memory_space=pltpu.HBM),
            pl.BlockSpec(memory_space=pltpu.HBM),
            pl.BlockSpec(memory_space=pltpu.HBM),
        ],
        out_specs=pl.BlockSpec(memory_space=pltpu.VMEM),
        scratch_shapes=[
            pltpu.VMEM(volume, F32),
            pltpu.VMEM(volume, F32),
            pltpu.VMEM(volume, F32),
            pltpu.VMEM((ITERS,) + volume, F32),
            pltpu.VMEM((ITERS,) + volume, F32),
            pltpu.VMEM((ITERS,) + volume, F32),
            pltpu.VMEM((2 * ITERS, 2, reach, planes, cols), F32),
            pltpu.VMEM((2 * ITERS, 2, rows, half, cols), F32),
            pltpu.VMEM((CHUNKS, rows + 2 * reach, chunk, cols), BF16),
            pltpu.VMEM((CHUNKS, rows + 2 * reach, chunk, cols), BF16),
            pltpu.VMEM((2, taps, 3 * cols, cols), BF16),
            pltpu.VMEM((2, 2 * planes, 2 * (planes + 2 * half)), BF16),
            pltpu.SMEM(lateral_psf.shape, F32),
            pltpu.SMEM(depth_psf.shape, F32),
            dma((2, rows)),
            dma((2,)),
            dma((2 * ITERS, 2, CHUNKS)),
            dma((2 * ITERS, 2, CHUNKS)),
            dma((ITERS, CHUNKS, groups)),
            dma((ITERS, CHUNKS, groups)),
            dma((ITERS, 2, groups)),
            dma((ITERS, 2, groups)),
        ],
        compiler_params=pltpu.CompilerParams(
            collective_id=0, has_side_effects=True, vmem_limit_bytes=63 * 1024 * 1024
        ),
        cost_estimate=pl.CostEstimate(
            flops=2 * 2 * ITERS * 3 * taps * planes * rows * cols * cols,
            bytes_accessed=3 * 4 * planes * rows * cols,
            transcendentals=0,
        ),
    )(observed, estimate, lateral_psf, depth_psf)
    return jnp.swapaxes(result, 0, 1)


def solution(mesh):
    return jax.shard_map(
        functools.partial(body, mesh.shape["xy"], mesh.shape["gz"]),
        mesh=mesh,
        in_specs=(P("gz", "xy", None), P("gz", "xy", None), P(), P()),
        out_specs=P("gz", "xy", None),
        check_vma=False,
    )
```
